32 devices in a mesh: groups: 2 (over x), sx: 8 (over z, y), sy: 2 (over core).
Axes of the slice: x: 2, y: 2, z: 4, core: 2. Of those that a mesh axis runs over, the one named last changes fastest.
Arguments:
- feature: bfloat16 [32, 64, 32, 128], P(('groups', 'sx'), 'sy'), parts along dimension 0, may hold values from -6 to 6
- weight_upper: bfloat16 [6912, 128], P('groups'), parts along dimension 0, may hold values from -0.109375 to 0.109375
- down_weight_matrix: bfloat16 [2048, 256], P('groups'), parts along dimension 0, may hold values from -0.1875 to 0.1875
- weight_lower: bfloat16 [13824, 256], P('groups'), parts along dimension 0, may hold values from -0.078125 to 0.078125
- cotangent: bfloat16 [16, 32, 16, 256], P(('groups', 'sx'), 'sy'), parts along dimension 0, may hold values from -6 to 6
Outputs:
- bottleneck: bfloat16 [16, 32, 16, 256], P(('groups', 'sx'), 'sy'), parts along dimension 0
- grad_feature: bfloat16 [32, 64, 32, 128], P(('groups', 'sx'), 'sy'), parts along dimension 0
- grad_upper: float32 [6912, 128], P(('groups', 'sx', 'sy')), parts along dimension 0
- down_weight_gradient: float32 [2048, 256], P(('groups', 'sx', 'sy')), parts along dimension 0
- grad_lower: float32 [13824, 256], P(('groups', 'sx', 'sy')), parts along dimension 0
The draws below stay inside these ranges and needn't reach their ends.
There are 2 independent parts, one for each index of `groups`. The reference program is written for one: setup_inputs(seed, part) draws one part's arguments, and reference() takes and returns one part's arrays. A program takes and returns all parts, laid end to end along the dimension named above; each array names one. Nothing has to cross between parts.
All inputs are finite; a program needn't handle non-finite values.
Results may differ from the reference program's by a relative error of at most 0.006.
Values may be sent and summed in bfloat16 or wider, within the bound.
A program may use at most 128 MiB of HBM per device.

```python
import jax
import jax.numpy as jnp
from jax import lax

C1 = 128
C2 = 256
ZA = 32
NXA = 16
NYA = 64
NXB = 8
NYB = 32
ZB = 16


def steps_of(rng, dims, split, low, largest):
    level, own = 1.0, jax.random.fold_in(rng, 6)
    for axis_at, parts in split:
        heights = jnp.exp(jax.random.uniform(jax.random.fold_in(own, axis_at), (parts,), jnp.float32, low / len(split), largest / len(split)))
        level = level * jnp.repeat(heights, dims[axis_at] // parts).reshape([-1 if axis == axis_at else 1 for axis in range(len(dims))])
    return level


def normal_values(stream_key, shape, spread, bound, pieces=(), held_as=jnp.bfloat16):
    entries = spread * jax.random.normal(stream_key, shape, jnp.float32)
    if pieces:
        entries = entries * steps_of(stream_key, shape, pieces, -0.22, 0.18)
    return jnp.clip(entries, -bound, bound).astype(held_as)


def setup_inputs(seed: int = 0, part: int = 0) -> dict:
    arg_keys = jax.random.split(jax.random.key(seed), 6)
    part_splits = jax.random.split(jax.random.fold_in(arg_keys[5], part), 6)
    return {
        "feature": normal_values(part_splits[0], (NXA, NYA, ZA, C1), 1.0, 6.0, ((0, 8), (1, 2))),
        "weight_upper": normal_values(part_splits[1], (27 * C1, C1), (27 * C1) ** -0.5, 0.109375),
        "down_weight_matrix": normal_values(part_splits[2], (8 * C1, C2), (8 * C1) ** -0.5, 0.1875),
        "weight_lower": normal_values(part_splits[3], (27 * C2, C2), (27 * C2) ** -0.5, 0.078125),
        "cotangent": normal_values(part_splits[4], (NXB, NYB, ZB, C2), 1.0, 6.0, ((0, 8), (1, 2))),
    }


def window(padded, tap_index, extent, direction):
    shift_x = direction * (tap_index // 9 - 1)
    shift_y = direction * (tap_index // 3 % 3 - 1)
    shift_z = direction * (tap_index % 3 - 1)
    return padded[1 + shift_x:1 + shift_x + extent[0], 1 + shift_y:1 + shift_y + extent[1], 1 + shift_z:1 + shift_z + extent[2]]

def activate(preact):
    return preact * jax.nn.sigmoid(preact)

def slope(preact):
    sigmoid_value = jax.nn.sigmoid(preact)
    return sigmoid_value * (1.0 + preact * (1.0 - sigmoid_value))

def pad_all(field):
    return jnp.pad(field, ((1, 1), (1, 1), (1, 1), (0, 0)))

def convolve(padded, weight_collection, extent):
    in_width = padded.shape[3]
    out_width = weight_collection.shape[1]
    kernel = weight_collection.reshape(in_width, 27, out_width)
    voxels = extent[0] * extent[1] * extent[2]
    summed = jnp.zeros((voxels, out_width), jnp.float32)
    for tap_index in range(27):
        window_rows = window(padded, tap_index, extent, 1).reshape(voxels, in_width)
        summed = summed + jnp.dot(window_rows, kernel[:, tap_index, :], preferred_element_type=jnp.float32)
    return summed.reshape(tuple(extent) + (out_width,))

def convolve_back(padded, weight_collection, extent):
    in_width = weight_collection.shape[0] // 27
    out_width = weight_collection.shape[1]
    kernel = weight_collection.reshape(in_width, 27, out_width)
    voxels = extent[0] * extent[1] * extent[2]
    summed = jnp.zeros((voxels, in_width), jnp.float32)
    for tap_index in range(27):
        window_rows = window(padded, tap_index, extent, -1).reshape(voxels, out_width)
        summed = summed + jnp.dot(window_rows, kernel[:, tap_index, :].T, preferred_element_type=jnp.float32)
    return summed.reshape(tuple(extent) + (in_width,))

def kernel_grad(padded, grads, extent):
    in_width = padded.shape[3]
    voxels = extent[0] * extent[1] * extent[2]
    flat_grads = grads.reshape(voxels, grads.shape[3])
    columns_list = []
    for tap_index in range(27):
        window_rows = window(padded, tap_index, extent, 1).reshape(voxels, in_width)
        columns_list.append(lax.dot_general(window_rows, flat_grads, (((0,), (0,)), ((), ())), preferred_element_type=jnp.float32))
    return jnp.stack(columns_list, axis=1).reshape(in_width * 27, flat_grads.shape[1])

def strided_reduce(finer_feature, weight_collection):
    in_width = finer_feature.shape[3]
    out_width = weight_collection.shape[1]
    kernel = weight_collection.reshape(in_width, 8, out_width)
    coarse_extent = (finer_feature.shape[0] // 2, finer_feature.shape[1] // 2, finer_feature.shape[2] // 2)
    voxels = coarse_extent[0] * coarse_extent[1] * coarse_extent[2]
    summed = jnp.zeros((voxels, out_width), jnp.float32)
    for corner in range(8):
        window_rows = finer_feature[corner // 4::2, corner // 2 % 2::2, corner % 2::2].reshape(voxels, in_width)
        summed = summed + jnp.dot(window_rows, kernel[:, corner, :], preferred_element_type=jnp.float32)
    return summed.reshape(coarse_extent + (out_width,))

def strided_reduce_adjoint(finer_feature, coarse_gradient, weight_collection):
    in_width = finer_feature.shape[3]
    out_width = weight_collection.shape[1]
    kernel = weight_collection.reshape(in_width, 8, out_width)
    coarse_extent = coarse_gradient.shape[:3]
    voxels = coarse_extent[0] * coarse_extent[1] * coarse_extent[2]
    flat_grads = coarse_gradient.reshape(voxels, out_width)
    data_list = []
    weight_list = []
    for corner in range(8):
        data_list.append(jnp.dot(flat_grads, kernel[:, corner, :].T, preferred_element_type=jnp.float32))
        window_rows = finer_feature[corner // 4::2, corner // 2 % 2::2, corner % 2::2].reshape(voxels, in_width)
        weight_list.append(lax.dot_general(window_rows, flat_grads, (((0,), (0,)), ((), ())), preferred_element_type=jnp.float32))
    stacked = jnp.stack(data_list, axis=0).reshape(2, 2, 2, coarse_extent[0], coarse_extent[1], coarse_extent[2], in_width)
    data_grad = stacked.transpose(3, 0, 4, 1, 5, 2, 6).reshape(finer_feature.shape)
    weight_grad = jnp.stack(weight_list, axis=1).reshape(in_width * 8, out_width)
    return (data_grad, weight_grad)

def reference(feature, weight_upper, down_weight_matrix, weight_lower, cotangent):
    extent_upper = feature.shape[:3]
    padded_feature = pad_all(feature)
    pre_upper = convolve(padded_feature, weight_upper, extent_upper)
    upper_hidden_feature = activate(pre_upper).astype(jnp.bfloat16)
    lower_preactivation = strided_reduce(upper_hidden_feature, down_weight_matrix)
    hidden_lower = activate(lower_preactivation).astype(jnp.bfloat16)
    extent_lower = hidden_lower.shape[:3]
    padded_lower = pad_all(hidden_lower)
    bottleneck = convolve(padded_lower, weight_lower, extent_lower).astype(jnp.bfloat16)
    grad_hidden_lower = convolve_back(pad_all(cotangent), weight_lower, extent_lower)
    lower_preact_gradient = (grad_hidden_lower * slope(lower_preactivation)).astype(jnp.bfloat16)
    grad_lower = kernel_grad(padded_lower, cotangent, extent_lower)
    upper_hidden_gradient, down_weight_gradient = strided_reduce_adjoint(upper_hidden_feature, lower_preact_gradient, down_weight_matrix)
    grad_pre_upper = (upper_hidden_gradient * slope(pre_upper)).astype(jnp.bfloat16)
    grad_upper = kernel_grad(padded_feature, grad_pre_upper, extent_upper)
    grad_feature = convolve_back(pad_all(grad_pre_upper), weight_upper, extent_upper).astype(jnp.bfloat16)
    return (bottleneck, grad_feature, grad_upper, down_weight_gradient, grad_lower)
```

```python
import functools

import jax
import jax.numpy as jnp
from jax import lax
from jax.experimental import pallas as pl
from jax.experimental.pallas import tpu as pltpu
from jax.sharding import PartitionSpec as P


def extended(block, sides, width):
    for axis, dim in sides:
        count = lax.axis_size(axis)
        forward = [(i, i + 1) for i in range(count - 1)]
        backward = [(target, source) for source, target in forward]
        low = lax.ppermute(
            lax.slice_in_dim(block, block.shape[dim] - width, None, axis=dim), axis, forward
        )
        high = lax.ppermute(lax.slice_in_dim(block, 0, width, axis=dim), axis, backward)
        block = jnp.concatenate([low, block, high], axis=dim)
    return block


def activate(preact):
    return preact * jax.nn.sigmoid(preact)


def slope(preact):
    sigmoid_value = jax.nn.sigmoid(preact)
    return sigmoid_value * (1.0 + preact * (1.0 - sigmoid_value))


def pad_depth(field):
    return jnp.pad(field, ((0, 0), (0, 0), (1, 1), (0, 0)))


def pad_upper(field):
    spread = extended(field, (("sx", 0), ("sy", 1)), 1)
    return pad_depth(spread)


def pad_lower(field):
    spread = extended(field, (("sx", 0), ("sy", 1)), 1)
    return pad_depth(spread)


def correlate(left, right, layout, strides, padding, left_dilation, right_dilation):
    return lax.conv_general_dilated(
        left,
        right,
        strides,
        padding,
        lhs_dilation=left_dilation,
        rhs_dilation=right_dilation,
        dimension_numbers=layout,
        preferred_element_type=jnp.float32,
    )


def convolve(padded, weight_collection):
    in_width = padded.shape[3]
    out_width = weight_collection.shape[1]
    kernel = weight_collection.reshape(in_width, 3, 3, 3, out_width)
    summed = correlate(
        padded[None],
        kernel,
        ("NDHWC", "IDHWO", "NDHWC"),
        (1, 1, 1),
        ((0, 0), (0, 0), (0, 0)),
        (1, 1, 1),
        (1, 1, 1),
    )
    return summed[0]


def convolve_back(padded, weight_collection):
    in_width = weight_collection.shape[0] // 27
    out_width = weight_collection.shape[1]
    kernel = weight_collection.reshape(in_width, 3, 3, 3, out_width)[:, ::-1, ::-1, ::-1, :]
    summed = correlate(
        padded[None],
        kernel,
        ("NDHWC", "ODHWI", "NDHWC"),
        (1, 1, 1),
        ((0, 0), (0, 0), (0, 0)),
        (1, 1, 1),
        (1, 1, 1),
    )
    return summed[0]


def kernel_grad(padded, grads):
    in_width = padded.shape[3]
    out_width = grads.shape[3]
    summed = correlate(
        padded[None],
        grads[..., None],
        ("CDHWN", "DHWOI", "NDHWC"),
        (1, 1, 1),
        ((0, 0), (0, 0), (0, 0)),
        (1, 1, 1),
        (1, 1, 1),
    )
    return summed.reshape(in_width * 27, out_width)


def strided_reduce(finer_feature, weight_collection):
    in_width = finer_feature.shape[3]
    out_width = weight_collection.shape[1]
    kernel = weight_collection.reshape(in_width, 2, 2, 2, out_width)
    summed = correlate(
        finer_feature[None],
        kernel,
        ("NDHWC", "IDHWO", "NDHWC"),
        (2, 2, 2),
        ((0, 0), (0, 0), (0, 0)),
        (1, 1, 1),
        (1, 1, 1),
    )
    return summed[0]


def strided_reduce_adjoint(finer_feature, coarse_gradient, weight_collection):
    in_width = finer_feature.shape[3]
    out_width = weight_collection.shape[1]
    kernel = weight_collection.reshape(in_width, 2, 2, 2, out_width)[:, ::-1, ::-1, ::-1, :]
    data_grad = correlate(
        coarse_gradient[None],
        kernel,
        ("NDHWC", "ODHWI", "NDHWC"),
        (1, 1, 1),
        ((1, 1), (1, 1), (1, 1)),
        (2, 2, 2),
        (1, 1, 1),
    )[0]
    weight_grad = correlate(
        finer_feature[None],
        coarse_gradient[..., None],
        ("CDHWN", "DHWOI", "NDHWC"),
        (1, 1, 1),
        ((0, 0), (0, 0), (0, 0)),
        (1, 1, 1),
        (2, 2, 2),
    )
    return (data_grad, weight_grad.reshape(in_width * 8, out_width))


def whole_volume(rows, extent):
    slabs_x = lax.axis_size("sx")
    slabs_y = lax.axis_size("sy")
    width = rows.shape[1]
    blocks = rows.reshape(slabs_x, slabs_y, extent[0], extent[1], extent[2], width)
    return blocks.transpose(0, 2, 1, 3, 4, 5).reshape(
        slabs_x * extent[0], slabs_y * extent[1], extent[2], width
    )


def body(feature, weight_upper, down_weight_matrix, weight_lower, cotangent):
    extent_lower = cotangent.shape[:3]
    lower_width = cotangent.shape[3]
    lower_voxels = extent_lower[0] * extent_lower[1] * extent_lower[2]
    cotangent_rows = lax.all_gather(
        cotangent.reshape(lower_voxels, lower_width), ("sx", "sy"), axis=0, tiled=True
    )
    padded_feature = pad_upper(feature)
    pre_upper = convolve(padded_feature, weight_upper)
    upper_hidden_feature = activate(pre_upper).astype(jnp.bfloat16)
    lower_preactivation = strided_reduce(upper_hidden_feature, down_weight_matrix)
    hidden_lower = activate(lower_preactivation).astype(jnp.bfloat16)
    padded_lower = pad_lower(hidden_lower)
    bottleneck = convolve(padded_lower, weight_lower).astype(jnp.bfloat16)
    owned_rows = lax.all_to_all(
        hidden_lower.reshape(lower_voxels, lower_width),
        ("sx", "sy"),
        split_axis=1,
        concat_axis=0,
        tiled=True,
    )
    grad_hidden_lower = convolve_back(pad_lower(cotangent), weight_lower)
    lower_preact_gradient = (grad_hidden_lower * slope(lower_preactivation)).astype(jnp.bfloat16)
    owned_volume = whole_volume(owned_rows, extent_lower)
    whole_cotangent = whole_volume(cotangent_rows, extent_lower)
    padded_owned = jnp.pad(owned_volume, ((1, 1), (1, 1), (1, 1), (0, 0)))
    lower_rows = kernel_grad(padded_owned, whole_cotangent)
    upper_hidden_gradient, downward_products = strided_reduce_adjoint(
        upper_hidden_feature, lower_preact_gradient, down_weight_matrix
    )
    grad_pre_upper = (upper_hidden_gradient * slope(pre_upper)).astype(jnp.bfloat16)
    upper_terms = kernel_grad(padded_feature, grad_pre_upper)
    grad_feature = convolve_back(pad_upper(grad_pre_upper), weight_upper).astype(jnp.bfloat16)
    down_rows, upper_rows = (
        lax.psum_scatter(downward_products, ("sx", "sy"), scatter_dimension=0, tiled=True),
        lax.psum_scatter(upper_terms, ("sx", "sy"), scatter_dimension=0, tiled=True),
    )
    return (bottleneck, grad_feature, upper_rows, down_rows, lower_rows)


BF, F32 = jnp.bfloat16, jnp.float32
MESH_ID = pl.DeviceIdType.MESH
NT = (((1,), (1,)), ((), ()))
TN = (((0,), (0,)), ((), ()))


def mm(left, right, dims=(((1,), (0,)), ((), ()))):
    return lax.dot_general(left, right, dims, preferred_element_type=F32)


def depth_taps(block, depth):
    wide = block.astype(F32)
    rows = wide.shape[0]
    at = lax.broadcasted_iota(jnp.int32, wide.shape, 0) % depth
    before = jnp.where(at == 0, 0.0, pltpu.roll(wide, 1, 0)).astype(BF)
    after = jnp.where(at == depth - 1, 0.0, pltpu.roll(wide, rows - 1, 0)).astype(BF)
    return before, block, after


def fused(n_sx, feat, wu, dw, wl, cot, bott, gfeat, gup, gdown, glow,
          fx, gx, hx, cx, call, ht, htr, xz, gz, hz, cz, wf, wb, wlf, wlb, wd, wtl, su, sd,
          pu, hu, gzt, hcat, ghl, pl_low, hp, at, gl, s1, r1, s2, r2,
          f_s, f_r, g_s, g_r, h_s, h_r, c_s, c_r, ca_s, ca_r, cf_s, cf_r, t_s, t_r,
          a_s, a_r, b_s, b_r):
    g, i, j = lax.axis_index("groups"), lax.axis_index("sx"), lax.axis_index("sy")
    k = 1 - j
    me = 2 * i + j
    total = 2 * n_sx

    def remote(src, dst, ss, rs, dev):
        return pltpu.make_async_remote_copy(
            src_ref=src, dst_ref=dst, send_sem=ss, recv_sem=rs, device_id=dev,
            device_id_type=MESH_ID)

    def guard(cond, f):
        if cond is None:
            f()
        else:
            pl.when(cond)(f)

    low, high = i > 0, i < n_sx - 1
    down_dev = lambda s: (g, jnp.maximum(i - 1, 0), s)
    up_dev = lambda s: (g, jnp.minimum(i + 1, n_sx - 1), s)

    def halo(buf, nx, ny, ss, rs):
        ysrc = ny - j * (ny - 1)
        ydst = j * (ny + 1)
        yrcv = k * (ny + 1)
        body = pl.ds(1, ny)
        slabs = pl.ds(1, nx)
        sends = [
            (low, buf.at[1, body], buf.at[nx + 1, body], down_dev(j)),
            (high, buf.at[nx, body], buf.at[0, body], up_dev(j)),
            (None, buf.at[slabs, ysrc], buf.at[slabs, ydst], (g, i, k)),
            (low, buf.at[1, ysrc], buf.at[nx + 1, ydst], down_dev(k)),
            (high, buf.at[nx, ysrc], buf.at[0, ydst], up_dev(k)),
        ]
        recvs = [
            (high, buf.at[nx + 1, body]),
            (low, buf.at[0, body]),
            (None, buf.at[slabs, yrcv]),
            (high, buf.at[nx + 1, yrcv]),
            (low, buf.at[0, yrcv]),
        ]

        def start():
            for m, (cond, src, dst, dev) in enumerate(sends):
                guard(cond, lambda m=m, src=src, dst=dst, dev=dev: remote(
                    src, dst, ss.at[m], rs.at[m], dev).start())

        def wait():
            for m, (cond, dst) in enumerate(recvs):
                guard(cond, lambda m=m, dst=dst: remote(
                    dst, dst, ss.at[m], rs.at[m], (g, i, k)).wait_recv())

        def done():
            for m, (cond, src, dst, dev) in enumerate(sends):
                guard(cond, lambda m=m, src=src, dst=dst, dev=dev: remote(
                    src, dst, ss.at[m], rs.at[m], dev).wait_send())

        return start, wait, done

    def edges(buf, nx, ny):
        zero_row = jnp.zeros(buf.shape[2:], BF)
        for s in range(nx + 2):
            buf[s, j * (ny + 1)] = zero_row

        @pl.when(i == 0)
        def _():
            buf[0] = jnp.zeros(buf.shape[1:], BF)

        @pl.when(i == n_sx - 1)
        def _():
            buf[nx + 1] = jnp.zeros(buf.shape[1:], BF)

    barrier = pltpu.get_barrier_semaphore()
    for q in range(1, total):
        other = lax.rem(me + q, total)
        pl.semaphore_signal(barrier, inc=1, device_id=(g, other // 2, other % 2),
                            device_id_type=MESH_ID)
    for s in range(2):
        fx[1 + s, 1:33] = feat[s]
    cx[1, 1:17] = cot[...].reshape(16, 16, 256)
    call[me] = cot[...]
    pl.semaphore_wait(barrier, total - 1)

    f_start, f_wait, f_done = halo(fx, 2, 32, f_s, f_r)
    g_start, g_wait, g_done = halo(gx, 2, 32, g_s, g_r)
    h_start, h_wait, h_done = halo(hx, 1, 16, h_s, h_r)
    c_start, c_wait, c_done = halo(cx, 1, 16, c_s, c_r)
    c_start()
    f_start()
    edges(fx, 2, 32)
    edges(gx, 2, 32)
    edges(hx, 1, 16)
    edges(cx, 1, 16)

    def widen_lower(s, _):
        rows = pl.ds(s * 256, 256)
        for h in range(2):
            wtl[h, rows] = wl[rows, h * 128:(h + 1) * 128].astype(F32)
        return 0
    lax.fori_loop(0, 27, widen_lower, 0)
    for t in range(27):
        for h in range(2):
            tap = wtl[h, pl.ds(t, 256, stride=27), :].astype(BF)
            e = t % 3
            wlf[t // 3, e * 256:(e + 1) * 256, h * 128:(h + 1) * 128] = tap
            u = 26 - t
            f = u % 3
            wlb[u // 3, :, f * 256 + h * 128:f * 256 + (h + 1) * 128] = tap

    c_wait()

    def lower_taps(src, dst):
        for s in range(3):
            parts = depth_taps(src[s].reshape(18 * 16, 256), 16)
            for e in range(3):
                dst[s, :, :, e * 256:(e + 1) * 256] = parts[e].reshape(18, 16, 256)
    lower_taps(cx, cz)
    acc = jnp.zeros((256, 256), F32)
    for ab in range(9):
        acc += mm(cz[ab // 3, ab % 3:ab % 3 + 16].reshape(256, 768), wlb[ab], NT)
    ghl[...] = acc

    su[...] = wu[...].astype(F32)
    for t in range(27):
        tap = su[pl.ds(t, 128, stride=27), :].astype(BF)
        e, u = t % 3, 26 - t
        f = u % 3
        wf[t // 3, e * 128:(e + 1) * 128, :] = tap
        wb[u // 3, :, f * 128:(f + 1) * 128] = tap
    for h in range(2):
        sd[h] = dw[:, h * 128:(h + 1) * 128].astype(F32)
    for c in range(8):
        for h in range(2):
            wd[c * 128:(c + 1) * 128, h * 128:(h + 1) * 128] = (
                sd[h, pl.ds(c, 128, stride=8), :].astype(BF))

    f_wait()

    def gather_copy(q):
        to = lax.rem(i + q, n_sx)
        return remote(call.at[me], call.at[me], ca_s.at[q], ca_r.at[q], (g, to, j))

    def gather_recv(q):
        frm = lax.rem(i - q + n_sx, n_sx)
        blk = call.at[2 * frm + j]
        return remote(blk, blk, ca_s.at[q], ca_r.at[q], (g, i, k))

    def forward_copy(q):
        frm = lax.rem(i - q + n_sx, n_sx)
        blk = call.at[2 * frm + j]
        return remote(blk, blk, cf_s.at[q], cf_r.at[q], (g, i, k))

    def forward_recv(q):
        frm = lax.rem(i - q + n_sx, n_sx)
        blk = call.at[2 * frm + k]
        return remote(blk, blk, cf_s.at[q], cf_r.at[q], (g, i, k))

    for q in range(1, n_sx):
        gather_copy(q).start()
    forward_copy(0).start()

    def upper_taps(src, dst, s, y0, ny):
        parts = depth_taps(src[s, pl.ds(y0, ny)].reshape(ny * 32, 128), 32)
        for e in range(3):
            dst[s, pl.ds(y0, ny), :, e * 128:(e + 1) * 128] = parts[e].reshape(ny, 32, 128)

    def upper_slab(s, _):
        upper_taps(fx, xz, s, 0, 34)
        return 0
    lax.fori_loop(0, 4, upper_slab, 0)

    def conv_up(m, _):
        s, y0 = m // 2, (m % 2) * 16
        acc = jnp.zeros((512, 128), F32)
        for ab in range(9):
            lhs = xz[s + ab // 3, pl.ds(y0 + ab % 3, 16)].reshape(512, 384)
            acc += mm(lhs, wf[ab])
        pu[s, pl.ds(y0, 16)] = acc.reshape(16, 32, 128)
        hid = (acc * jax.nn.sigmoid(acc)).astype(BF).astype(F32)
        hu[s, pl.ds(y0 // 2, 8)] = hid.reshape(8, 2, 32, 128)
        return 0
    lax.fori_loop(0, 4, conv_up, 0)

    for c in range(8):
        ii, jj, ll = c // 4, c // 2 % 2, c % 2
        hcat[:, c * 128:(c + 1) * 128] = (
            hu[ii, :, jj, pl.ds(ll, 16, stride=2), :].reshape(256, 128).astype(BF))
    pre = mm(hcat[...], wd[...])
    sig = jax.nn.sigmoid(pre)
    hid_low = pre * sig
    ht[...] = hid_low.T.astype(BF)
    hx[1, 1:17] = hid_low.astype(BF).reshape(16, 16, 256)
    gpl = (ghl[...] * (sig * (1.0 + pre * (1.0 - sig)))).astype(BF)
    pl_low[...] = gpl
    h_start()

    def turn_copy(q):
        other = lax.rem(me + q, total)
        return remote(ht.at[pl.ds(16 * other, 16)], htr.at[me], t_s.at[q], t_r.at[q],
                      (g, other // 2, other % 2))

    def turn_recv(q):
        frm = lax.rem(me - q + total, total)
        return remote(htr.at[frm], htr.at[frm], t_s.at[q], t_r.at[q], (g, i, k))
    for q in range(1, total):
        turn_copy(q).start()
    htr[me] = ht[pl.ds(pl.multiple_of(16 * me, 16), 16)]

    for c in range(8):
        ii, jj, ll = c // 4, c // 2 % 2, c % 2
        back = mm(gpl, wd[c * 128:(c + 1) * 128, :], NT)
        hu[ii, :, jj, pl.ds(ll, 16, stride=2), :] = back.reshape(16, 16, 128)

    def grad_pre(m, _):
        s, y0 = m // 4, (m % 4) * 8
        v = pu[s, pl.ds(y0, 8)]
        sg = jax.nn.sigmoid(v)
        grad = hu[s, pl.ds(y0 // 2, 4)].reshape(8, 32, 128) * (sg * (1.0 + v * (1.0 - sg)))
        gx[s + 1, pl.ds(y0 + 1, 8)] = grad.astype(BF)
        return 0
    lax.fori_loop(0, 8, grad_pre, 0)
    g_start()

    for s in range(2):
        upper_taps(gx, gz, s + 1, 1, 32)
        for e in range(3):
            col = gz[s + 1, 1:33, :, e * 128:(e + 1) * 128].reshape(1024, 128)
            gzt[e * 128:(e + 1) * 128, s * 1024:(s + 1) * 1024] = col.T

    dgrad = mm(hcat[...], pl_low[...], TN)
    for c in range(8):
        for h in range(2):
            sd[h, pl.ds(c, 128, stride=8), :] = dgrad[c * 128:(c + 1) * 128, h * 128:(h + 1) * 128]
    for ab in range(9):
        acc = jnp.zeros((384, 128), F32)
        for s in range(2):
            rhs = fx[s + ab // 3, ab % 3:ab % 3 + 32].reshape(1024, 128)
            acc += mm(gzt[:, s * 1024:(s + 1) * 1024], rhs)
        for e in range(3):
            t = ab * 3 + 2 - e
            su[pl.ds(t, 128, stride=27), :] = acc[e * 128:(e + 1) * 128].T

    for d in range(total):
        q, s = d // 2, d % 2
        s1[s, q, 0:216] = su[216 * d:216 * (d + 1)].astype(BF)
        s1[s, q, 216:224] = jnp.zeros((8, 128), BF)
        s1[s, q, 224:288] = sd[0, 64 * d:64 * (d + 1)].astype(BF)
        s1[s, q, 288:352] = sd[1, 64 * d:64 * (d + 1)].astype(BF)
    pair = remote(s1.at[k], r1, a_s, a_r, (g, i, k))
    pair.start()

    h_wait()
    lower_taps(hx, hz)
    acc = jnp.zeros((256, 256), F32)
    for ab in range(9):
        acc += mm(hz[ab // 3, ab % 3:ab % 3 + 16].reshape(256, 768), wlf[ab])
    bott[...] = acc.astype(BF)

    pair.wait_recv()
    for q in range(n_sx):
        s2[q] = (s1[j, q].astype(F32) + r1[q].astype(F32)).astype(BF)

    def sum_copy(q):
        to = lax.rem(i + q, n_sx)
        return remote(s2.at[to], r2.at[q], b_s.at[q], b_r.at[q], (g, to, j))
    for q in range(1, n_sx):
        sum_copy(q).start()

    for q in range(1, n_sx):
        gather_recv(q).wait_recv()
        forward_copy(q).start()

    g_wait()
    upper_taps(gx, gz, 0, 0, 34)
    upper_taps(gx, gz, 3, 0, 34)
    for s in (1, 2):
        for y in (0, 33):
            upper_taps(gx, gz, s, y, 1)

    def conv_down(m, _):
        s, y0 = m // 2, (m % 2) * 16
        acc = jnp.zeros((512, 128), F32)
        for ab in range(9):
            lhs = gz[s + ab // 3, pl.ds(y0 + ab % 3, 16)].reshape(512, 384)
            acc += mm(lhs, wb[ab], NT)
        gfeat[s, pl.ds(y0, 16)] = acc.astype(BF).reshape(16, 32, 128)
        return 0
    lax.fori_loop(0, 4, conv_down, 0)

    for q in range(1, total):
        turn_recv(q).wait_recv()
    hp[...] = jnp.zeros(hp.shape, F32)
    for d in range(total):
        hp[:, 640 + 256 * d:640 + 256 * (d + 1)] = htr[d].astype(F32)
    lane = lax.broadcasted_iota(jnp.int32, (16, 5120), 1)
    z, y = lane % 16, lane // 16 % 32
    for be in range(9):
        b, e = be // 3 - 1, be % 3 - 1
        shift = 16 * b + e
        moved = pltpu.roll(hp[...], (-shift) % 5376, 1)[:, 128:5248]
        ok = (z + e >= 0) & (z + e < 16) & (y + b >= 0) & (y + b < 32)
        moved = jnp.where(ok, moved, 0.0).astype(BF)
        for a in range(3):
            t = a * 9 + be
            at[t * 16:(t + 1) * 16, :] = moved[:, 512 * a:512 * a + 4096]
    for q in range(n_sx):
        forward_recv(q).wait_recv()
    acc = jnp.zeros((432, 256), F32)
    for c in range(4):
        acc += mm(at[:, c * 1024:(c + 1) * 1024], call[4 * c:4 * c + 4].reshape(1024, 256))
    for t in range(27):
        for h in range(2):
            gl[h, pl.ds(t, 16, stride=27), :] = acc[t * 16:(t + 1) * 16, h * 128:(h + 1) * 128]
    for h in range(2):
        glow[:, h * 128:(h + 1) * 128] = gl[h]

    rows = s2[i].astype(F32)
    for q in range(1, n_sx):
        blk = r2.at[q]
        remote(blk, blk, b_s.at[q], b_r.at[q], (g, i, k)).wait_recv()
        rows += r2[q].astype(F32)
    gup[...] = rows[0:216]
    gdown[:, 0:128] = rows[224:288]
    gdown[:, 128:256] = rows[288:352]

    f_done()
    g_done()
    h_done()
    c_done()
    pair.wait_send()
    for q in range(1, n_sx):
        gather_copy(q).wait_send()
        sum_copy(q).wait_send()
    for q in range(n_sx):
        forward_copy(q).wait_send()
    for q in range(1, total):
        turn_copy(q).wait_send()


def fused_body(feature, weight_upper, down_weight_matrix, weight_lower, cotangent):
    n_sx = lax.axis_size("sx")
    total = 2 * n_sx
    V = pltpu.VMEM
    S = pltpu.SemaphoreType.DMA
    scratch = [
        V((4, 34, 32, 128), BF), V((4, 34, 32, 128), BF), V((3, 18, 16, 256), BF),
        V((3, 18, 16, 256), BF), V((total, 256, 256), BF), V((256, 256), BF),
        V((total, 16, 256), BF), V((4, 34, 32, 384), BF), V((4, 34, 32, 384), BF),
        V((3, 18, 16, 768), BF), V((3, 18, 16, 768), BF),
        V((9, 384, 128), BF), V((9, 128, 384), BF), V((9, 768, 256), BF), V((9, 256, 768), BF),
        V((1024, 256), BF), V((2, 6912, 128), F32), V((3456, 128), F32), V((2, 1024, 128), F32),
        V((2, 32, 32, 128), F32), V((2, 16, 2, 32, 128), F32), V((384, 2048), BF),
        V((256, 1024), BF), V((256, 256), F32), V((256, 256), BF),
        V((16, 5376), F32), V((432, 4096), BF), V((2, 432, 128), F32),
        V((2, n_sx, 352, 128), BF), V((n_sx, 352, 128), BF), V((n_sx, 352, 128), BF),
        V((n_sx, 352, 128), BF),
        S((5,)), S((5,)), S((5,)), S((5,)), S((5,)), S((5,)), S((5,)), S((5,)),
        S((n_sx,)), S((n_sx,)), S((n_sx,)), S((n_sx,)), S((total,)), S((total,)),
        S, S, S((n_sx,)), S((n_sx,)),
    ]
    vm = pl.BlockSpec(memory_space=pltpu.VMEM)
    bott, gfeat, gup, gdown, glow = pl.pallas_call(
        functools.partial(fused, n_sx),
        out_shape=(
            jax.ShapeDtypeStruct((256, 256), BF),
            jax.ShapeDtypeStruct((2, 32, 32, 128), BF),
            jax.ShapeDtypeStruct((216, 128), F32),
            jax.ShapeDtypeStruct((64, 256), F32),
            jax.ShapeDtypeStruct((432, 256), F32),
        ),
        in_specs=[vm] * 5,
        out_specs=(vm,) * 5,
        scratch_shapes=scratch,
        compiler_params=pltpu.CompilerParams(
            collective_id=0, has_side_effects=True, vmem_limit_bytes=60 * 1024 * 1024),
        cost_estimate=pl.CostEstimate(flops=9_000_000_000, bytes_accessed=12_000_000,
                                      transcendentals=600_000),
    )(feature, weight_upper, down_weight_matrix, weight_lower, cotangent.reshape(256, 256))
    return (bott.reshape(1, 16, 16, 256), gfeat, gup, gdown, glow)


def solution(mesh):
    placed = (
        P(("groups", "sx"), "sy", None, None),
        P("groups", None),
        P("groups", None),
        P("groups", None),
        P(("groups", "sx"), "sy", None, None),
    )
    fits = mesh.shape["sx"] == 8 and mesh.shape["sy"] == 2
    return jax.shard_map(
        fused_body if fits else body,
        mesh=mesh,
        in_specs=placed,
        out_specs=(
            P(("groups", "sx"), "sy", None, None),
            P(("groups", "sx"), "sy", None, None),
            P(("groups", "sx", "sy"), None),
            P(("groups", "sx", "sy"), None),
            P(("groups", "sx", "sy"), None),
        ),
        check_vma=False,
    )
```

```python
import functools

import jax
import jax.numpy as jnp
from jax import lax
from jax.experimental import pallas as pl
from jax.experimental.pallas import tpu as pltpu
from jax.sharding import PartitionSpec as P


def extended(block, sides, width):
    for axis, dim in sides:
        count = lax.axis_size(axis)
        forward = [(i, i + 1) for i in range(count - 1)]
        backward = [(target, source) for source, target in forward]
        low = lax.ppermute(
            lax.slice_in_dim(block, block.shape[dim] - width, None, axis=dim), axis, forward
        )
        high = lax.ppermute(lax.slice_in_dim(block, 0, width, axis=dim), axis, backward)
        block = jnp.concatenate([low, block, high], axis=dim)
    return block


def activate(preact):
    return preact * jax.nn.sigmoid(preact)


def slope(preact):
    sigmoid_value = jax.nn.sigmoid(preact)
    return sigmoid_value * (1.0 + preact * (1.0 - sigmoid_value))


def pad_depth(field):
    return jnp.pad(field, ((0, 0), (0, 0), (1, 1), (0, 0)))


def pad_upper(field):
    spread = extended(field, (("sx", 0), ("sy", 1)), 1)
    return pad_depth(spread)


def pad_lower(field):
    spread = extended(field, (("sx", 0), ("sy", 1)), 1)
    return pad_depth(spread)


def correlate(left, right, layout, strides, padding, left_dilation, right_dilation):
    return lax.conv_general_dilated(
        left,
        right,
        strides,
        padding,
        lhs_dilation=left_dilation,
        rhs_dilation=right_dilation,
        dimension_numbers=layout,
        preferred_element_type=jnp.float32,
    )


def convolve(padded, weight_collection):
    in_width = padded.shape[3]
    out_width = weight_collection.shape[1]
    kernel = weight_collection.reshape(in_width, 3, 3, 3, out_width)
    summed = correlate(
        padded[None],
        kernel,
        ("NDHWC", "IDHWO", "NDHWC"),
        (1, 1, 1),
        ((0, 0), (0, 0), (0, 0)),
        (1, 1, 1),
        (1, 1, 1),
    )
    return summed[0]


def convolve_back(padded, weight_collection):
    in_width = weight_collection.shape[0] // 27
    out_width = weight_collection.shape[1]
    kernel = weight_collection.reshape(in_width, 3, 3, 3, out_width)[:, ::-1, ::-1, ::-1, :]
    summed = correlate(
        padded[None],
        kernel,
        ("NDHWC", "ODHWI", "NDHWC"),
        (1, 1, 1),
        ((0, 0), (0, 0), (0, 0)),
        (1, 1, 1),
        (1, 1, 1),
    )
    return summed[0]


def kernel_grad(padded, grads):
    in_width = padded.shape[3]
    out_width = grads.shape[3]
    summed = correlate(
        padded[None],
        grads[..., None],
        ("CDHWN", "DHWOI", "NDHWC"),
        (1, 1, 1),
        ((0, 0), (0, 0), (0, 0)),
        (1, 1, 1),
        (1, 1, 1),
    )
    return summed.reshape(in_width * 27, out_width)


def strided_reduce(finer_feature, weight_collection):
    in_width = finer_feature.shape[3]
    out_width = weight_collection.shape[1]
    kernel = weight_collection.reshape(in_width, 2, 2, 2, out_width)
    summed = correlate(
        finer_feature[None],
        kernel,
        ("NDHWC", "IDHWO", "NDHWC"),
        (2, 2, 2),
        ((0, 0), (0, 0), (0, 0)),
        (1, 1, 1),
        (1, 1, 1),
    )
    return summed[0]


def strided_reduce_adjoint(finer_feature, coarse_gradient, weight_collection):
    in_width = finer_feature.shape[3]
    out_width = weight_collection.shape[1]
    kernel = weight_collection.reshape(in_width, 2, 2, 2, out_width)[:, ::-1, ::-1, ::-1, :]
    data_grad = correlate(
        coarse_gradient[None],
        kernel,
        ("NDHWC", "ODHWI", "NDHWC"),
        (1, 1, 1),
        ((1, 1), (1, 1), (1, 1)),
        (2, 2, 2),
        (1, 1, 1),
    )[0]
    weight_grad = correlate(
        finer_feature[None],
        coarse_gradient[..., None],
        ("CDHWN", "DHWOI", "NDHWC"),
        (1, 1, 1),
        ((0, 0), (0, 0), (0, 0)),
        (1, 1, 1),
        (2, 2, 2),
    )
    return (data_grad, weight_grad.reshape(in_width * 8, out_width))


def whole_volume(rows, extent):
    slabs_x = lax.axis_size("sx")
    slabs_y = lax.axis_size("sy")
    width = rows.shape[1]
    blocks = rows.reshape(slabs_x, slabs_y, extent[0], extent[1], extent[2], width)
    return blocks.transpose(0, 2, 1, 3, 4, 5).reshape(
        slabs_x * extent[0], slabs_y * extent[1], extent[2], width
    )


def body(feature, weight_upper, down_weight_matrix, weight_lower, cotangent):
    extent_lower = cotangent.shape[:3]
    lower_width = cotangent.shape[3]
    lower_voxels = extent_lower[0] * extent_lower[1] * extent_lower[2]
    cotangent_rows = lax.all_gather(
        cotangent.reshape(lower_voxels, lower_width), ("sx", "sy"), axis=0, tiled=True
    )
    padded_feature = pad_upper(feature)
    pre_upper = convolve(padded_feature, weight_upper)
    upper_hidden_feature = activate(pre_upper).astype(jnp.bfloat16)
    lower_preactivation = strided_reduce(upper_hidden_feature, down_weight_matrix)
    hidden_lower = activate(lower_preactivation).astype(jnp.bfloat16)
    padded_lower = pad_lower(hidden_lower)
    bottleneck = convolve(padded_lower, weight_lower).astype(jnp.bfloat16)
    owned_rows = lax.all_to_all(
        hidden_lower.reshape(lower_voxels, lower_width),
        ("sx", "sy"),
        split_axis=1,
        concat_axis=0,
        tiled=True,
    )
    grad_hidden_lower = convolve_back(pad_lower(cotangent), weight_lower)
    lower_preact_gradient = (grad_hidden_lower * slope(lower_preactivation)).astype(jnp.bfloat16)
    owned_volume = whole_volume(owned_rows, extent_lower)
    whole_cotangent = whole_volume(cotangent_rows, extent_lower)
    padded_owned = jnp.pad(owned_volume, ((1, 1), (1, 1), (1, 1), (0, 0)))
    lower_rows = kernel_grad(padded_owned, whole_cotangent)
    upper_hidden_gradient, downward_products = strided_reduce_adjoint(
        upper_hidden_feature, lower_preact_gradient, down_weight_matrix
    )
    grad_pre_upper = (upper_hidden_gradient * slope(pre_upper)).astype(jnp.bfloat16)
    upper_terms = kernel_grad(padded_feature, grad_pre_upper)
    grad_feature = convolve_back(pad_upper(grad_pre_upper), weight_upper).astype(jnp.bfloat16)
    down_rows, upper_rows = (
        lax.psum_scatter(downward_products, ("sx", "sy"), scatter_dimension=0, tiled=True),
        lax.psum_scatter(upper_terms, ("sx", "sy"), scatter_dimension=0, tiled=True),
    )
    return (bottleneck, grad_feature, upper_rows, down_rows, lower_rows)


BF, F32 = jnp.bfloat16, jnp.float32
MESH_ID = pl.DeviceIdType.MESH
NT = (((1,), (1,)), ((), ()))
TN = (((0,), (0,)), ((), ()))


def mm(left, right, dims=(((1,), (0,)), ((), ()))):
    return lax.dot_general(left, right, dims, preferred_element_type=F32)


def depth_taps(block, depth):
    wide = block.astype(F32)
    rows = wide.shape[0]
    at = lax.broadcasted_iota(jnp.int32, wide.shape, 0) % depth
    before = jnp.where(at == 0, 0.0, pltpu.roll(wide, 1, 0)).astype(BF)
    after = jnp.where(at == depth - 1, 0.0, pltpu.roll(wide, rows - 1, 0)).astype(BF)
    return before, block, after


def fused(n_sx, feat, wu, dw, wl, cot, bott, gfeat, gup, gdown, glow,
          fx, gx, hx, cx, call, ht, htr, xz, gz, hz, cz, wf, wb, wlf, wlb, wd, wtl, su, sd,
          pu, hu, gzt, hcat, ghl, pl_low, hp, at, gl, s1, r1, s2, ry, s3, r2,
          f_s, f_r, g_s, g_r, h_s, h_r, c_s, c_r, ca_s, ca_r, cf_s, cf_r, t_s, t_r,
          a_s, a_r, b_s, b_r, y_s, y_r, m_s, m_r):
    g, i, j = lax.axis_index("groups"), lax.axis_index("sx"), lax.axis_index("sy")
    k = 1 - j
    me = 2 * i + j
    total = 2 * n_sx

    def remote(src, dst, ss, rs, dev):
        return pltpu.make_async_remote_copy(
            src_ref=src, dst_ref=dst, send_sem=ss, recv_sem=rs, device_id=dev,
            device_id_type=MESH_ID)

    def guard(cond, f):
        if cond is None:
            f()
        else:
            pl.when(cond)(f)

    low, high = i > 0, i < n_sx - 1
    down_dev = lambda s: (g, jnp.maximum(i - 1, 0), s)
    up_dev = lambda s: (g, jnp.minimum(i + 1, n_sx - 1), s)

    def halo(buf, nx, ny, ss, rs):
        ysrc = ny - j * (ny - 1)
        ydst = j * (ny + 1)
        yrcv = k * (ny + 1)
        body = pl.ds(1, ny)
        slabs = pl.ds(1, nx)
        sends = [
            (low, buf.at[1, body], buf.at[nx + 1, body], down_dev(j)),
            (high, buf.at[nx, body], buf.at[0, body], up_dev(j)),
            (None, buf.at[slabs, ysrc], buf.at[slabs, ydst], (g, i, k)),
            (low, buf.at[1, ysrc], buf.at[nx + 1, ydst], down_dev(k)),
            (high, buf.at[nx, ysrc], buf.at[0, ydst], up_dev(k)),
        ]
        recvs = [
            (high, buf.at[nx + 1, body]),
            (low, buf.at[0, body]),
            (None, buf.at[slabs, yrcv]),
            (high, buf.at[nx + 1, yrcv]),
            (low, buf.at[0, yrcv]),
        ]

        def start():
            for m, (cond, src, dst, dev) in enumerate(sends):
                guard(cond, lambda m=m, src=src, dst=dst, dev=dev: remote(
                    src, dst, ss.at[m], rs.at[m], dev).start())

        def wait():
            for m, (cond, dst) in enumerate(recvs):
                guard(cond, lambda m=m, dst=dst: remote(
                    dst, dst, ss.at[m], rs.at[m], (g, i, k)).wait_recv())

        def done():
            for m, (cond, src, dst, dev) in enumerate(sends):
                guard(cond, lambda m=m, src=src, dst=dst, dev=dev: remote(
                    src, dst, ss.at[m], rs.at[m], dev).wait_send())

        return start, wait, done

    def edges(buf, nx, ny):
        zero_row = jnp.zeros(buf.shape[2:], BF)
        for s in range(nx + 2):
            buf[s, j * (ny + 1)] = zero_row

        @pl.when(i == 0)
        def _():
            buf[0] = jnp.zeros(buf.shape[1:], BF)

        @pl.when(i == n_sx - 1)
        def _():
            buf[nx + 1] = jnp.zeros(buf.shape[1:], BF)

    barrier = pltpu.get_barrier_semaphore()
    for q in range(1, total):
        other = lax.rem(me + q, total)
        pl.semaphore_signal(barrier, inc=1, device_id=(g, other // 2, other % 2),
                            device_id_type=MESH_ID)
    for s in range(2):
        fx[1 + s, 1:33] = feat[s]
    cx[1, 1:17] = cot[...].reshape(16, 16, 256)
    call[me] = cot[...]
    pl.semaphore_wait(barrier, total - 1)

    f_start, f_wait, f_done = halo(fx, 2, 32, f_s, f_r)
    g_start, g_wait, g_done = halo(gx, 2, 32, g_s, g_r)
    h_start, h_wait, h_done = halo(hx, 1, 16, h_s, h_r)
    c_start, c_wait, c_done = halo(cx, 1, 16, c_s, c_r)
    c_start()
    f_start()

    nz = n_sx // 2
    zc, yc = i // 2, i % 2
    mate = i + 1 - 2 * yc
    part_copy = remote(call.at[me], call.at[me], y_s, y_r, (g, mate, j))
    part_copy.start()

    def hop(way, step, p):
        src = zc - step if way == 0 else zc + step
        inside = src >= 0 if way == 0 else src < nz
        more = zc < nz - 1 if way == 0 else zc > 0
        blk = call.at[2 * (2 * jnp.clip(src, 0, nz - 1) + p) + j]
        to = jnp.clip(i + 2 if way == 0 else i - 2, 0, n_sx - 1)
        slot = way * n_sx + step * 2 + p
        return inside & more, inside, remote(blk, blk, ca_s.at[slot], ca_r.at[slot], (g, to, j))

    def landed(way, step, p):
        src = zc - step if way == 0 else zc + step
        inside = src >= 0 if way == 0 else src < nz
        blk = call.at[2 * (2 * jnp.clip(src, 0, nz - 1) + p) + j]
        slot = way * n_sx + (step - 1) * 2 + p
        return inside, remote(blk, blk, ca_s.at[slot], ca_r.at[slot], (g, i, k))

    def chain(step):
        for way in range(2):
            for p in range(2):
                if step:
                    inside, got = landed(way, step, p)
                    guard(inside, got.wait_recv)
                if step < nz - 1:
                    go, _, copy = hop(way, step, p)
                    guard(go, copy.start)

    def forward_copy(q):
        blk = call.at[2 * q + j]
        return remote(blk, blk, cf_s.at[q], cf_r.at[q], (g, i, k))

    def forward_recv(q):
        blk = call.at[2 * q + k]
        return remote(blk, blk, cf_s.at[q], cf_r.at[q], (g, i, k))

    edges(fx, 2, 32)
    edges(gx, 2, 32)
    edges(hx, 1, 16)
    edges(cx, 1, 16)

    def widen_lower(s, _):
        rows = pl.ds(s * 256, 256)
        for h in range(2):
            wtl[h, rows] = wl[rows, h * 128:(h + 1) * 128].astype(F32)
        return 0
    lax.fori_loop(0, 27, widen_lower, 0)
    for t in range(27):
        for h in range(2):
            tap = wtl[h, pl.ds(t, 256, stride=27), :].astype(BF)
            e = t % 3
            wlf[t // 3, e * 256:(e + 1) * 256, h * 128:(h + 1) * 128] = tap
            u = 26 - t
            f = u % 3
            wlb[u // 3, :, f * 256 + h * 128:f * 256 + (h + 1) * 128] = tap

    c_wait()

    def lower_taps(src, dst):
        for s in range(3):
            parts = depth_taps(src[s].reshape(18 * 16, 256), 16)
            for e in range(3):
                dst[s, :, :, e * 256:(e + 1) * 256] = parts[e].reshape(18, 16, 256)
    lower_taps(cx, cz)
    acc = jnp.zeros((256, 256), F32)
    for ab in range(9):
        acc += mm(cz[ab // 3, ab % 3:ab % 3 + 16].reshape(256, 768), wlb[ab], NT)
    ghl[...] = acc

    su[...] = wu[...].astype(F32)
    for t in range(27):
        tap = su[pl.ds(t, 128, stride=27), :].astype(BF)
        e, u = t % 3, 26 - t
        f = u % 3
        wf[t // 3, e * 128:(e + 1) * 128, :] = tap
        wb[u // 3, :, f * 128:(f + 1) * 128] = tap
    for h in range(2):
        sd[h] = dw[:, h * 128:(h + 1) * 128].astype(F32)
    for c in range(8):
        for h in range(2):
            wd[c * 128:(c + 1) * 128, h * 128:(h + 1) * 128] = (
                sd[h, pl.ds(c, 128, stride=8), :].astype(BF))

    f_wait()

    part_copy.wait_recv()
    chain(0)

    def upper_taps(src, dst, s, y0, ny):
        parts = depth_taps(src[s, pl.ds(y0, ny)].reshape(ny * 32, 128), 32)
        for e in range(3):
            dst[s, pl.ds(y0, ny), :, e * 128:(e + 1) * 128] = parts[e].reshape(ny, 32, 128)

    def upper_slab(s, _):
        upper_taps(fx, xz, s, 0, 34)
        return 0
    lax.fori_loop(0, 4, upper_slab, 0)

    def conv_up(m, _):
        s, y0 = m // 2, (m % 2) * 16
        acc = jnp.zeros((512, 128), F32)
        for ab in range(9):
            lhs = xz[s + ab // 3, pl.ds(y0 + ab % 3, 16)].reshape(512, 384)
            acc += mm(lhs, wf[ab])
        pu[s, pl.ds(y0, 16)] = acc.reshape(16, 32, 128)
        hid = (acc * jax.nn.sigmoid(acc)).astype(BF).astype(F32)
        hu[s, pl.ds(y0 // 2, 8)] = hid.reshape(8, 2, 32, 128)
        return 0
    lax.fori_loop(0, 4, conv_up, 0)

    for c in range(8):
        ii, jj, ll = c // 4, c // 2 % 2, c % 2
        hcat[:, c * 128:(c + 1) * 128] = (
            hu[ii, :, jj, pl.ds(ll, 16, stride=2), :].reshape(256, 128).astype(BF))
    pre = mm(hcat[...], wd[...])
    sig = jax.nn.sigmoid(pre)
    hid_low = pre * sig
    ht[...] = hid_low.T.astype(BF)
    hx[1, 1:17] = hid_low.astype(BF).reshape(16, 16, 256)
    gpl = (ghl[...] * (sig * (1.0 + pre * (1.0 - sig)))).astype(BF)
    pl_low[...] = gpl
    h_start()

    def turn_copy(q):
        other = lax.rem(me + q, total)
        return remote(ht.at[pl.ds(16 * other, 16)], htr.at[me], t_s.at[q], t_r.at[q],
                      (g, other // 2, other % 2))

    def turn_recv(q):
        frm = lax.rem(me - q + total, total)
        return remote(htr.at[frm], htr.at[frm], t_s.at[q], t_r.at[q], (g, i, k))
    for q in range(1, total):
        turn_copy(q).start()
    htr[me] = ht[pl.ds(pl.multiple_of(16 * me, 16), 16)]

    for c in range(8):
        ii, jj, ll = c // 4, c // 2 % 2, c % 2
        back = mm(gpl, wd[c * 128:(c + 1) * 128, :], NT)
        hu[ii, :, jj, pl.ds(ll, 16, stride=2), :] = back.reshape(16, 16, 128)

    def grad_pre(m, _):
        s, y0 = m // 4, (m % 4) * 8
        v = pu[s, pl.ds(y0, 8)]
        sg = jax.nn.sigmoid(v)
        grad = hu[s, pl.ds(y0 // 2, 4)].reshape(8, 32, 128) * (sg * (1.0 + v * (1.0 - sg)))
        gx[s + 1, pl.ds(y0 + 1, 8)] = grad.astype(BF)
        return 0
    lax.fori_loop(0, 8, grad_pre, 0)
    g_start()
    chain(1)

    for s in range(2):
        upper_taps(gx, gz, s + 1, 1, 32)
        for e in range(3):
            col = gz[s + 1, 1:33, :, e * 128:(e + 1) * 128].reshape(1024, 128)
            gzt[e * 128:(e + 1) * 128, s * 1024:(s + 1) * 1024] = col.T

    dgrad = mm(hcat[...], pl_low[...], TN)
    for c in range(8):
        for h in range(2):
            sd[h, pl.ds(c, 128, stride=8), :] = dgrad[c * 128:(c + 1) * 128, h * 128:(h + 1) * 128]
    for ab in range(9):
        acc = jnp.zeros((384, 128), F32)
        for s in range(2):
            rhs = fx[s + ab // 3, ab % 3:ab % 3 + 32].reshape(1024, 128)
            acc += mm(gzt[:, s * 1024:(s + 1) * 1024], rhs)
        for e in range(3):
            t = ab * 3 + 2 - e
            su[pl.ds(t, 128, stride=27), :] = acc[e * 128:(e + 1) * 128].T

    for d in range(total):
        q, s = d // 2, d % 2
        s1[s, q, 0:216] = su[216 * d:216 * (d + 1)].astype(BF)
        s1[s, q, 216:224] = jnp.zeros((8, 128), BF)
        s1[s, q, 224:288] = sd[0, 64 * d:64 * (d + 1)].astype(BF)
        s1[s, q, 288:352] = sd[1, 64 * d:64 * (d + 1)].astype(BF)
    pair = remote(s1.at[k], r1, a_s, a_r, (g, i, k))
    pair.start()

    h_wait()
    lower_taps(hx, hz)
    acc = jnp.zeros((256, 256), F32)
    for ab in range(9):
        acc += mm(hz[ab // 3, ab % 3:ab % 3 + 16].reshape(256, 768), wlf[ab])
    bott[...] = acc.astype(BF)

    pair.wait_recv()
    for q in range(n_sx):
        s2[q % 2, q // 2] = (s1[j, q].astype(F32) + r1[q].astype(F32)).astype(BF)
    mate_copy = remote(s2.at[1 - yc], ry, m_s, m_r, (g, mate, j))
    mate_copy.start()
    chain(2)

    g_wait()
    upper_taps(gx, gz, 0, 0, 34)
    upper_taps(gx, gz, 3, 0, 34)
    for s in (1, 2):
        for y in (0, 33):
            upper_taps(gx, gz, s, y, 1)

    def conv_down(m, _):
        s, y0 = m // 2, (m % 2) * 16
        acc = jnp.zeros((512, 128), F32)
        for ab in range(9):
            lhs = gz[s + ab // 3, pl.ds(y0 + ab % 3, 16)].reshape(512, 384)
            acc += mm(lhs, wb[ab], NT)
        gfeat[s, pl.ds(y0, 16)] = acc.astype(BF).reshape(16, 32, 128)
        return 0
    lax.fori_loop(0, 4, conv_down, 0)

    mate_copy.wait_recv()
    for q in range(nz):
        s3[q] = (s2[yc, q].astype(F32) + ry[q].astype(F32)).astype(BF)

    def sum_copy(q):
        to = lax.rem(zc + q, nz)
        return remote(s3.at[to], r2.at[q], b_s.at[q], b_r.at[q], (g, 2 * to + yc, j))
    for q in range(1, nz):
        sum_copy(q).start()
    chain(3)
    for q in range(n_sx):
        forward_copy(q).start()

    for q in range(1, total):
        turn_recv(q).wait_recv()
    hp[...] = jnp.zeros(hp.shape, F32)
    for d in range(total):
        hp[:, 640 + 256 * d:640 + 256 * (d + 1)] = htr[d].astype(F32)
    lane = lax.broadcasted_iota(jnp.int32, (16, 5120), 1)
    z, y = lane % 16, lane // 16 % 32
    for be in range(9):
        b, e = be // 3 - 1, be % 3 - 1
        shift = 16 * b + e
        moved = pltpu.roll(hp[...], (-shift) % 5376, 1)[:, 128:5248]
        ok = (z + e >= 0) & (z + e < 16) & (y + b >= 0) & (y + b < 32)
        moved = jnp.where(ok, moved, 0.0).astype(BF)
        for a in range(3):
            t = a * 9 + be
            at[t * 16:(t + 1) * 16, :] = moved[:, 512 * a:512 * a + 4096]
    for q in range(n_sx):
        forward_recv(q).wait_recv()
    acc = jnp.zeros((432, 256), F32)
    for c in range(4):
        acc += mm(at[:, c * 1024:(c + 1) * 1024], call[4 * c:4 * c + 4].reshape(1024, 256))
    for t in range(27):
        for h in range(2):
            gl[h, pl.ds(t, 16, stride=27), :] = acc[t * 16:(t + 1) * 16, h * 128:(h + 1) * 128]
    for h in range(2):
        glow[:, h * 128:(h + 1) * 128] = gl[h]

    rows = s3[zc].astype(F32)
    for q in range(1, nz):
        blk = r2.at[q]
        remote(blk, blk, b_s.at[q], b_r.at[q], (g, i, k)).wait_recv()
        rows += r2[q].astype(F32)
    gup[...] = rows[0:216]
    gdown[:, 0:128] = rows[224:288]
    gdown[:, 128:256] = rows[288:352]

    f_done()
    g_done()
    h_done()
    c_done()
    pair.wait_send()
    part_copy.wait_send()
    mate_copy.wait_send()
    for q in range(1, nz):
        sum_copy(q).wait_send()
    for way in range(2):
        for step in range(nz - 1):
            for p in range(2):
                go, _, copy = hop(way, step, p)
                guard(go, copy.wait_send)
    for q in range(n_sx):
        forward_copy(q).wait_send()
    for q in range(1, total):
        turn_copy(q).wait_send()


def hand_on(*refs):
    sems = refs[10]
    copies = [pltpu.make_async_copy(refs[m], refs[5 + m], sems.at[m]) for m in range(5)]
    for copy in copies:
        copy.start()
    for copy in copies:
        copy.wait()


def fused_body(feature, weight_upper, down_weight_matrix, weight_lower, cotangent):
    n_sx = lax.axis_size("sx")
    total = 2 * n_sx
    V = pltpu.VMEM
    S = pltpu.SemaphoreType.DMA
    scratch = [
        V((4, 34, 32, 128), BF), V((4, 34, 32, 128), BF), V((3, 18, 16, 256), BF),
        V((3, 18, 16, 256), BF), V((total, 256, 256), BF), V((256, 256), BF),
        V((total, 16, 256), BF), V((4, 34, 32, 384), BF), V((4, 34, 32, 384), BF),
        V((3, 18, 16, 768), BF), V((3, 18, 16, 768), BF),
        V((9, 384, 128), BF), V((9, 128, 384), BF), V((9, 768, 256), BF), V((9, 256, 768), BF),
        V((1024, 256), BF), V((2, 6912, 128), F32), V((3456, 128), F32), V((2, 1024, 128), F32),
        V((2, 32, 32, 128), F32), V((2, 16, 2, 32, 128), F32), V((384, 2048), BF),
        V((256, 1024), BF), V((256, 256), F32), V((256, 256), BF),
        V((16, 5376), F32), V((432, 4096), BF), V((2, 432, 128), F32),
        V((2, n_sx, 352, 128), BF), V((n_sx, 352, 128), BF), V((2, n_sx // 2, 352, 128), BF),
        V((n_sx // 2, 352, 128), BF), V((n_sx // 2, 352, 128), BF), V((n_sx // 2, 352, 128), BF),
        S((5,)), S((5,)), S((5,)), S((5,)), S((5,)), S((5,)), S((5,)), S((5,)),
        S((2 * n_sx,)), S((2 * n_sx,)), S((n_sx,)), S((n_sx,)), S((total,)), S((total,)),
        S, S, S((n_sx,)), S((n_sx,)), S, S, S, S,
    ]
    vm = pl.BlockSpec(memory_space=pltpu.VMEM)
    bott, gfeat, gup, gdown, glow = pl.pallas_call(
        functools.partial(fused, n_sx),
        out_shape=(
            jax.ShapeDtypeStruct((256, 256), BF),
            jax.ShapeDtypeStruct((2, 32, 32, 128), BF),
            jax.ShapeDtypeStruct((216, 128), F32),
            jax.ShapeDtypeStruct((64, 256), F32),
            jax.ShapeDtypeStruct((432, 256), F32),
        ),
        in_specs=[vm] * 5,
        out_specs=(vm,) * 5,
        scratch_shapes=scratch,
        compiler_params=pltpu.CompilerParams(
            collective_id=0, has_side_effects=True, vmem_limit_bytes=60 * 1024 * 1024),
        cost_estimate=pl.CostEstimate(flops=9_000_000_000, bytes_accessed=12_000_000,
                                      transcendentals=600_000),
    )(feature, weight_upper, down_weight_matrix, weight_lower, cotangent.reshape(256, 256))
    results = (bott, gfeat, gup, gdown, glow)
    anywhere = pl.BlockSpec(memory_space=pl.ANY)
    bott, gfeat, gup, gdown, glow = pl.pallas_call(
        hand_on,
        out_shape=tuple(jax.ShapeDtypeStruct(r.shape, r.dtype) for r in results),
        in_specs=[anywhere] * 5,
        out_specs=(anywhere,) * 5,
        scratch_shapes=[S((5,))],
    )(*results)
    return (bott.reshape(1, 16, 16, 256), gfeat, gup, gdown, glow)


def solution(mesh):
    placed = (
        P(("groups", "sx"), "sy", None, None),
        P("groups", None),
        P("groups", None),
        P("groups", None),
        P(("groups", "sx"), "sy", None, None),
    )
    fits = mesh.shape["sx"] == 8 and mesh.shape["sy"] == 2
    return jax.shard_map(
        fused_body if fits else body,
        mesh=mesh,
        in_specs=placed,
        out_specs=(
            P(("groups", "sx"), "sy", None, None),
            P(("groups", "sx"), "sy", None, None),
            P(("groups", "sx", "sy"), None),
            P(("groups", "sx", "sy"), None),
            P(("groups", "sx", "sy"), None),
        ),
        check_vma=False,
    )
```
